32 devices in a mesh: rx: 8 (over z, core), ry: 4 (over y, x).
Axes of the slice: x: 2, y: 2, z: 4, core: 2. Of those that a mesh axis runs over, the one named last changes fastest.
Arguments:
- primal: bfloat16 [4096, 320], P(('rx', 'ry')), may hold values from -6 to 6
- adjoint: bfloat16 [4096, 320], P(('rx', 'ry')), may hold values from -6 to 6
- send_index: int32 [128, 16], P(('rx', 'ry')), may hold values from 0 to 127, as said below
- neighbours: int32 [4096, 6], P(('rx', 'ry')), may hold values from 0 to 191, as said below
- recon: bfloat16 [7, 64, 125], replicated, may hold values from -0.25 to 0.25
- deriv: bfloat16 [3, 125, 125], replicated, may hold values from -0.5 to 0.5
- jacob: float32 [3, 5, 5], replicated, may hold values from -3 to 3
- face_trace: bfloat16 [125, 150], replicated, may hold values from -0.5 to 0.5
- lift: bfloat16 [150, 125], replicated, may hold values from -0.5 to 0.5
- dissip: float32 [5], replicated, may hold values from 0.5 to 2
Outputs:
- indicators: float32 [4096], P(('rx', 'ry'))
The draws below stay inside these ranges and needn't reach their ends.
Inputs may be any that keep to these rules, and one draw needn't show every extreme that they name: `send_index`: each row lists 16 different local elements of its region. `neighbours`: an entry below 128 is a local element of the element's region; an entry 128 + d * 16 + j appears only at face f = d and only where the region in direction d exists; at a face on the outer boundary the entry is below 128.
All inputs are finite; a program needn't handle non-finite values.
Results may differ from the reference program's by a relative error of at most 0.004.
Values may be sent and summed in bfloat16 or wider, within the bound.
No kernel may reach another device: no remote copies, remote signals or barrier semaphores. Data moves between devices by JAX's collectives and lax.ppermute only.
A program may use at most 128 MiB of HBM per device.

```python
import math
import jax
import jax.numpy as jnp
from jax import lax

E_DEV = 128
VARS = 5
MODES = 64
ENR = 125
FACEPTS = 25
FACES = 6
PATCH = 7
S = 16
ELEMS = 4096
N_RX = 8
N_RY = 4


def draw_send_index(key, part):
    keys = jax.random.split(jax.random.fold_in(key, 11), N_RX * N_RY * 4)

    def listing(sub):
        return jax.random.permutation(sub, E_DEV)[:S]
    return jax.vmap(listing)(keys).astype(jnp.int32)


def draw_neighbours(key, part):
    base = jax.random.fold_in(key, 23)
    key_local, key_cross, key_slot = jax.random.split(base, 3)
    local_pick = jax.random.randint(key_local, (ELEMS, FACES), 0, E_DEV)
    crossing = jax.random.randint(key_cross, (ELEMS, FACES), 0, 4) == 0
    slot = jax.random.randint(key_slot, (ELEMS, FACES), 0, S)
    elem = jnp.arange(ELEMS, dtype=jnp.int32)
    device = elem // E_DEV
    own = (elem % E_DEV)[:, None]
    row_ix = device // N_RY
    col_iy = device % N_RY
    never = jnp.zeros_like(row_ix) > 0
    exists = jnp.stack([row_ix > 0, row_ix < N_RX - 1, col_iy > 0, col_iy < N_RY - 1, never, never], axis=1)
    face = jnp.arange(FACES, dtype=jnp.int32)[None, :]
    halo_row = E_DEV + face * S + slot
    picked = jnp.where(crossing & exists, halo_row, jnp.where(crossing, own, local_pick))
    return picked.astype(jnp.int32)


def levels(key, extent, shards, low, largest):
    gain = 1.0
    for dim, parts in shards:
        steps = jax.random.uniform(jax.random.fold_in(jax.random.fold_in(key, 6), dim), (parts,), jnp.float32, low / len(shards), largest / len(shards))
        gain = gain * jnp.repeat(jnp.exp(steps), extent[dim] // parts).reshape((-1,) + (1,) * (len(extent) - 1 - dim))
    return gain


def normal_values(rng, extent, spread, bound, shards=(), kind=jnp.bfloat16):
    gain = levels(rng, extent, shards, -0.22, 0.18) if shards else 1.0
    entries = jax.random.normal(rng, extent, jnp.float32) * spread * gain
    return jnp.minimum(jnp.maximum(entries, -bound), bound).astype(kind)


def setup_inputs(seed: int = 0) -> dict:
    key_of = jax.random.split(jax.random.key(seed), 11)
    return {
        "primal": normal_values(key_of[0], (ELEMS, VARS * MODES), 1.0, 6.0, ((0, 32),)),
        "adjoint": normal_values(key_of[1], (ELEMS, VARS * MODES), 1.0, 6.0, ((0, 32),)),
        "send_index": draw_send_index(jax.random.fold_in(key_of[10], 71), 0),
        "neighbours": draw_neighbours(jax.random.fold_in(key_of[10], 71), 0),
        "recon": normal_values(key_of[4], (PATCH, MODES, ENR), (PATCH * MODES) ** -0.5, 0.25),
        "deriv": normal_values(key_of[5], (3, ENR, ENR), ENR ** -0.5, 0.5),
        "jacob": normal_values(key_of[6], (3, VARS, VARS), 0.5, 3.0, (), jnp.float32),
        "face_trace": normal_values(key_of[7], (ENR, FACES * FACEPTS), ENR ** -0.5, 0.5),
        "lift": normal_values(key_of[8], (FACES * FACEPTS, ENR), (FACES * FACEPTS) ** -0.5, 0.5),
        "dissip": jnp.clip(jnp.exp(jax.random.uniform(key_of[9], (VARS,), jnp.float32, math.log(0.5), math.log(2.0))), 0.5, 2.0),
    }


def global_rows(send_index, neighbours):
    elem = jnp.arange(ELEMS, dtype=jnp.int32)
    device = elem // E_DEV
    row_ix = device // N_RY
    col_iy = device % N_RY
    entry = neighbours
    halo = entry - E_DEV
    direction = jnp.clip(halo // S, 0, 3).astype(jnp.int32)
    slot = jnp.clip(halo % S, 0, S - 1).astype(jnp.int32)
    step_x = jnp.array([-1, 1, 0, 0], dtype=jnp.int32)[direction]
    step_y = jnp.array([0, 0, -1, 1], dtype=jnp.int32)[direction]
    sender = jnp.clip(row_ix[:, None] + step_x, 0, N_RX - 1) * N_RY + jnp.clip(col_iy[:, None] + step_y, 0, N_RY - 1)
    sent_row = send_index[sender * 4 + jnp.bitwise_xor(direction, 1), slot]
    local_id = device[:, None] * E_DEV + entry
    remote_id = sender * E_DEV + sent_row
    return jnp.where(entry < E_DEV, local_id, remote_id).astype(jnp.int32)


def enrich(field, members, recon):
    count = members.shape[0]
    total = jnp.zeros((count, VARS, ENR), jnp.float32)
    for k in range(PATCH):
        rows = field[members[:, k]].reshape(count, VARS, MODES).astype(jnp.float32)
        total = total + jnp.einsum('evm,mn->evn', rows, recon[k].astype(jnp.float32))
    return total


def reference(primal, adjoint, send_index, neighbours, recon, deriv, jacob, face_trace, lift, dissip):
    face_ids = global_rows(send_index, neighbours)
    self_ids = jnp.arange(ELEMS, dtype=jnp.int32)[:, None]
    patch_ids = jnp.concatenate([self_ids, face_ids], axis=1)
    blocks = N_RX * N_RY

    def first_pass(block):
        members = lax.dynamic_slice_in_dim(patch_ids, block * E_DEV, E_DEV, 0)
        u4b = enrich(primal, members, recon).astype(jnp.bfloat16)
        traces = jnp.einsum('evn,nq->evq', u4b.astype(jnp.float32), face_trace.astype(jnp.float32)).astype(jnp.bfloat16)
        return u4b, traces

    u4_all, traces_all = lax.map(first_pass, jnp.arange(blocks, dtype=jnp.int32))
    u4_all = u4_all.reshape(ELEMS, VARS, ENR)
    traces_all = traces_all.reshape(ELEMS, VARS, FACES, FACEPTS)
    signs = jnp.array([-1.0, 1.0, -1.0, 1.0, -1.0, 1.0], dtype=jnp.float32)
    face_jacob = jnp.repeat(jacob, 2, axis=0) * (0.5 * signs)[:, None, None]

    def second_pass(block):
        start = block * E_DEV
        members = lax.dynamic_slice_in_dim(patch_ids, start, E_DEV, 0)
        z4 = enrich(adjoint, members, recon)
        u4b = lax.dynamic_slice_in_dim(u4_all, start, E_DEV, 0)
        inner = lax.dynamic_slice_in_dim(traces_all, start, E_DEV, 0).astype(jnp.float32)
        across = members[:, 1:]
        outer = jnp.stack([traces_all[across[:, f], :, f ^ 1, :] for f in range(FACES)], axis=2).astype(jnp.float32)
        mixed = jnp.einsum('fvw,ewfq->evfq', face_jacob, inner + outer, precision=lax.Precision.HIGHEST)
        flux = (mixed + 0.5 * dissip[None, :, None, None] * (inner - outer)).astype(jnp.bfloat16)
        volume = jnp.zeros((E_DEV, VARS, ENR), jnp.float32)
        for a in range(3):
            grad = jnp.einsum('evn,nm->evm', u4b.astype(jnp.float32), deriv[a].astype(jnp.float32))
            volume = volume + jnp.einsum('vw,ewm->evm', jacob[a], grad, precision=lax.Precision.HIGHEST)
        lifted = jnp.einsum('evq,qm->evm', flux.reshape(E_DEV, VARS, FACES * FACEPTS).astype(jnp.float32), lift.astype(jnp.float32))
        residual = volume - lifted
        return 0.04 * jnp.sum(z4 * residual, axis=(1, 2))

    return lax.map(second_pass, jnp.arange(blocks, dtype=jnp.int32)).reshape(ELEMS)
```

```python
import functools

import jax
import jax.numpy as jnp
from jax import lax
from jax.experimental import pallas as pl
from jax.experimental.pallas import tpu as pltpu
from jax.sharding import PartitionSpec as P

VARS = 5
MODES = 64
ENR = 125
FACEPTS = 25
FACES = 6
PATCH = 7
LANE = 128
TILES = 5
AXES = ("rx", "ry")
F32 = jnp.float32
BF16 = jnp.bfloat16
VMEM_BYTES = 16 * 1024 * 1024
PRIMAL_AT = ((0, 0), (0, 1), (1, 0), (1, 1), (4, 0))
ADJOINT_AT = ((2, 0), (2, 1), (3, 0), (3, 1), (4, 1))


def swaps(nx, ny):
    def joint(i, j):
        return i * ny + j

    def both(a, b):
        return [(a, b), (b, a)]

    x_even, x_odd, y_even, y_odd = [], [], [], []
    for j in range(ny):
        for i in range(0, nx - 1, 2):
            x_even += both(joint(i, j), joint(i + 1, j))
        for i in range(1, nx - 1, 2):
            x_odd += both(joint(i, j), joint(i + 1, j))
    for i in range(nx):
        for j in range(0, ny - 1, 2):
            y_even += both(joint(i, j), joint(i, j + 1))
        for j in range(1, ny - 1, 2):
            y_odd += both(joint(i, j), joint(i, j + 1))
    for i in {0, nx - 1 if nx % 2 == 0 else 0}:
        for j in range(0, ny - 1, 2):
            x_odd += both(joint(i, j), joint(i, j + 1))
    for j in {0, ny - 1 if ny % 2 == 0 else 0}:
        for i in range(0, nx - 1, 2):
            y_odd += both(joint(i, j), joint(i + 1, j))
    return x_even, x_odd, y_even, y_odd


def parities():
    odd_x = lax.rem(lax.axis_index("rx"), 2)
    odd_y = lax.rem(lax.axis_index("ry"), 2)
    return 1 - odd_x, odd_x, 3 - odd_y, 2 + odd_y


def listed(send_ref, faces):
    sent = send_ref.shape[1]
    rows = [
        jnp.broadcast_to(send_ref[pl.ds(face, 1), :], (sent, sent)) for face in faces
    ]
    table = jnp.concatenate(rows, axis=0)
    lane = lax.broadcasted_iota(jnp.int32, table.shape, 1)
    row = lax.rem(lax.broadcasted_iota(jnp.int32, table.shape, 0), sent)
    column = jnp.sum(jnp.where(lane == row, table, 0).astype(F32), axis=1, keepdims=True)
    return column.astype(jnp.int32)


def onehot(column, width, base):
    lane = lax.broadcasted_iota(jnp.int32, (column.shape[0], width), 1) + base
    return jnp.where(lane == column, 1.0, 0.0).astype(BF16)


def pick(nbr, face):
    lane = lax.broadcasted_iota(jnp.int32, nbr.shape, 1)
    return jnp.sum(jnp.where(lane == face, nbr, 0).astype(F32), axis=1, keepdims=True).astype(jnp.int32)


def dot(a, b):
    return jnp.dot(a, b, preferred_element_type=F32)


def dot_t(a, b):
    return lax.dot_general(a, b, (((1,), (1,)), ((), ())), preferred_element_type=F32)


def pack_kernel(primal_ref, adjoint_ref, send_ref, both_ref, *out_refs):
    sent = send_ref.shape[1]
    primal = primal_ref[...]
    adjoint = adjoint_ref[...]
    both = jnp.concatenate(
        [primal[:, 0:256], adjoint[:, 0:256], primal[:, 256:320], adjoint[:, 256:320]], axis=1
    )
    both_ref[...] = both
    pickings = onehot(listed(send_ref, parities()), primal.shape[0], 0)
    rows = dot(pickings, both).astype(BF16)
    for j, out_ref in enumerate(out_refs):
        out_ref[...] = rows[j * sent : (j + 1) * sent]


def local_kernel(both_ref, nbr_ref, recon_ref, acc_ref, weights_ref, left_ref):
    count = both_ref.shape[0]
    weights_ref[...] = jnp.zeros_like(weights_ref)
    for k in range(PATCH):
        weights_ref[k, 0:MODES, 0:ENR] = recon_ref[k]
        weights_ref[k, MODES : 2 * MODES, LANE : LANE + ENR] = recon_ref[k]
    both = both_ref[...]
    for k in range(PATCH):
        if k == 0:
            rows = both
        else:
            rows = dot(onehot(nbr_ref[:, k - 1 : k], count, 0), both).astype(BF16)
        for t in range(TILES):
            left_ref[t * count : (t + 1) * count, k * LANE : (k + 1) * LANE] = rows[:, t * LANE : (t + 1) * LANE]
    acc_ref[...] = dot(left_ref[...], weights_ref[...].reshape(PATCH * LANE, 2 * LANE))


def enrich_kernel(acc_ref, weights_ref, nbr_ref, send_ref, a_ref, b_ref, c_ref, d_ref, u_ref, z_ref, *out_refs):
    count, sent = nbr_ref.shape[0], send_ref.shape[1]
    faces = parities()
    nbr = nbr_ref[...]
    acc = acc_ref[...]
    for face, ref in zip(faces, (a_ref, b_ref, c_ref, d_ref)):
        hot = onehot(pick(nbr, face), sent, count + face * sent)
        rows = dot(hot, ref[...]).astype(BF16)
        left = jnp.concatenate([rows[:, t * LANE : (t + 1) * LANE] for t in range(TILES)], axis=0)
        acc = acc + dot(left, weights_ref[face + 1])
    for v in range(VARS):
        t, h = PRIMAL_AT[v]
        u_ref[:, v * LANE : (v + 1) * LANE] = acc[t * count : (t + 1) * count, h * LANE : (h + 1) * LANE].astype(BF16)
        t, h = ADJOINT_AT[v]
        z_ref[v * count : (v + 1) * count, :] = acc[t * count : (t + 1) * count, h * LANE : (h + 1) * LANE]
    pickings = onehot(listed(send_ref, faces), count, 0)
    rows = dot(pickings, u_ref[...]).astype(BF16)
    for j, out_ref in enumerate(out_refs):
        out_ref[...] = rows[j * sent : (j + 1) * sent]


def split(x):
    high = x.astype(BF16)
    return high, (x - high.astype(F32)).astype(BF16)


def middle_kernel(
    u_ref, z_ref, nbr_ref, deriv_ref, jacob_ref, trace_ref, lift_ref, dissip_ref, part_ref, c_ref, wide_ref, lift_pad, trace_pad
):
    count = nbr_ref.shape[0]
    points = FACES * FACEPTS
    wide_ref[...] = jnp.zeros_like(wide_ref)
    lift_pad[...] = jnp.zeros_like(lift_pad)
    trace_pad[...] = jnp.zeros_like(trace_pad)
    for a in range(3):
        wide_ref[0:ENR, a * LANE : a * LANE + ENR] = deriv_ref[a]
    wide_ref[0:ENR, 3 * LANE : 3 * LANE + points] = trace_ref[...]
    lift_pad[0:points, 0:ENR] = lift_ref[...]
    trace_pad[0:ENR, 0:points] = trace_ref[...].astype(F32)
    u = u_ref[...]
    stack = jnp.concatenate([u[:, v * LANE : (v + 1) * LANE] for v in range(VARS)], axis=0)
    grads = dot(stack, wide_ref[...])
    z = z_ref[...]
    z_high, z_low = split(z)
    lifted = dot_t(z_high, lift_pad[...]) + dot_t(z_low, lift_pad[...])

    def of(x, v):
        return x[v * count : (v + 1) * count]

    part = jnp.zeros((count, LANE), F32)
    for a in range(3):
        for w in range(VARS):
            zj = jacob_ref[a, 0, w] * of(z, 0)
            for v in range(1, VARS):
                zj = zj + jacob_ref[a, v, w] * of(z, v)
            part = part + zj * of(grads, w)[:, a * LANE : (a + 1) * LANE]
    lane = lax.broadcasted_iota(jnp.int32, (1, 2 * LANE), 1)
    face = lane // FACEPTS
    half = jnp.where(lax.rem(face, 2) == 0, -0.5, 0.5)
    outer_weights = []
    for w in range(VARS):
        mixed = None
        for v in range(VARS):
            coef = half * jnp.where(face < 2, jacob_ref[0, v, w], jnp.where(face < 4, jacob_ref[1, v, w], jacob_ref[2, v, w]))
            term = coef * of(lifted, v)
            mixed = term if mixed is None else mixed + term
        damped = (0.5 * dissip_ref[w]) * of(lifted, w)
        inner = of(grads, w)[:, 3 * LANE :] * (mixed + damped)
        part = part - inner[:, 0:LANE] - inner[:, LANE:]
        outer_weights.append(mixed - damped)
    b_high, b_low = split(jnp.concatenate(outer_weights, axis=0))
    plain = trace_pad[...]
    swapped = jnp.where(
        lax.rem(face, 2) == 0, pltpu.roll(plain, 2 * LANE - FACEPTS, 1), pltpu.roll(plain, FACEPTS, 1)
    )
    blocks = jnp.concatenate([jnp.where(face == f, swapped, 0.0).astype(BF16) for f in range(FACES)], axis=0)
    coef = dot_t(b_high, blocks) + dot_t(b_low, blocks)
    for f in range(FACES):
        mine = coef[:, f * LANE : (f + 1) * LANE]
        rows = dot(onehot(nbr_ref[:, f : f + 1], count, 0), u)
        for v in range(VARS):
            part = part - rows[:, v * LANE : (v + 1) * LANE] * of(mine, v)
        if f < 4:
            c_ref[f] = mine
    part_ref[...] = part


def last_kernel(part_ref, coef_ref, nbr_ref, a_ref, b_ref, c_ref, d_ref, out_ref):
    count, sent = nbr_ref.shape[0], a_ref.shape[0]
    nbr = nbr_ref[...]
    part = part_ref[...]
    for face, ref in zip(parities(), (a_ref, b_ref, c_ref, d_ref)):
        hot = onehot(pick(nbr, face), sent, count + face * sent)
        rows = dot(hot, ref[...])
        coef = coef_ref[face]
        for v in range(VARS):
            part = part - rows[:, v * LANE : (v + 1) * LANE] * coef[v * count : (v + 1) * count]
    out_ref[...] = 0.04 * jnp.sum(part.T, axis=0, keepdims=True)


def call(kernel, outs, specs=None, scratch=(), flops=0, moved=0):
    def run(*args):
        places = specs or [pltpu.VMEM] * len(args)
        return pl.pallas_call(
            kernel,
            out_shape=outs,
            in_specs=[pl.BlockSpec(memory_space=m) for m in places],
            out_specs=jax.tree.map(lambda _: pl.BlockSpec(memory_space=pltpu.VMEM), outs),
            scratch_shapes=scratch,
            compiler_params=pltpu.CompilerParams(vmem_limit_bytes=VMEM_BYTES),
            cost_estimate=pl.CostEstimate(flops=flops, bytes_accessed=moved, transcendentals=0),
        )(*args)

    return run


def shards(mesh, primal, adjoint, send_index, neighbours, recon, deriv, jacob, face_trace, lift, dissip):
    count, sent = primal.shape[0], send_index.shape[1]
    perms = swaps(mesh.shape["rx"], mesh.shape["ry"])
    wide = TILES * LANE
    shape = jax.ShapeDtypeStruct
    message = shape((sent, wide), BF16)
    both, *first = call(pack_kernel, [shape((count, wide), BF16)] + [message] * 4)(primal, adjoint, send_index)
    got = [lax.ppermute(m, AXES, pairs) for m, pairs in zip(first, perms)]
    acc, weights = call(
        local_kernel,
        [shape((TILES * count, 2 * LANE), F32), shape((PATCH, LANE, 2 * LANE), BF16)],
        scratch=[pltpu.VMEM((TILES * count, PATCH * LANE), BF16)],
        flops=10**9,
        moved=10**6,
    )(both, neighbours, recon)
    u4, z4, *second = call(
        enrich_kernel, [shape((count, wide), BF16), shape((VARS * count, LANE), F32)] + [message] * 4
    )(acc, weights, neighbours, send_index, *got)
    got = [lax.ppermute(m, AXES, pairs) for m, pairs in zip(second, perms)]
    smem, vmem = pltpu.SMEM, pltpu.VMEM
    part, coef = call(
        middle_kernel,
        [shape((count, LANE), F32), shape((4, VARS * count, LANE), F32)],
        specs=[vmem, vmem, vmem, vmem, smem, vmem, vmem, smem],
        scratch=[
            pltpu.VMEM((LANE, 5 * LANE), BF16),
            pltpu.VMEM((2 * LANE, LANE), BF16),
            pltpu.VMEM((LANE, 2 * LANE), F32),
        ],
        flops=10**9,
        moved=10**6,
    )(u4, z4, neighbours, deriv, jacob, face_trace, lift, dissip)
    out = call(last_kernel, shape((1, count), F32))(part, coef, neighbours, *got)
    return out.reshape(count)


def solution(mesh):
    rows = P(AXES, None)
    return jax.shard_map(
        functools.partial(shards, mesh),
        mesh=mesh,
        in_specs=(rows, rows, rows, rows, P(), P(), P(), P(), P(), P()),
        out_specs=P(AXES),
        check_vma=False,
    )
```

```python
import functools

import jax
import jax.numpy as jnp
from jax import lax
from jax.experimental import pallas as pl
from jax.experimental.pallas import tpu as pltpu
from jax.sharding import PartitionSpec as P

VARS = 5
MODES = 64
ENR = 125
FACEPTS = 25
FACES = 6
PATCH = 7
LANE = 128
WIDE = VARS * LANE
FIELD = VARS * MODES
POINTS = FACES * FACEPTS
AXES = ("rx", "ry")
F32 = jnp.float32
BF16 = jnp.bfloat16
VMEM_BYTES = 16 * 1024 * 1024


def swaps(nx, ny):
    def joint(i, j):
        return i * ny + j

    def both(a, b):
        return [(a, b), (b, a)]

    x_even, x_odd, y_even, y_odd = [], [], [], []
    for j in range(ny):
        for i in range(0, nx - 1, 2):
            x_even += both(joint(i, j), joint(i + 1, j))
        for i in range(1, nx - 1, 2):
            x_odd += both(joint(i, j), joint(i + 1, j))
    for i in range(nx):
        for j in range(0, ny - 1, 2):
            y_even += both(joint(i, j), joint(i, j + 1))
        for j in range(1, ny - 1, 2):
            y_odd += both(joint(i, j), joint(i, j + 1))
    for i in {0, nx - 1 if nx % 2 == 0 else 0}:
        for j in range(0, ny - 1, 2):
            x_odd += both(joint(i, j), joint(i, j + 1))
    for j in {0, ny - 1 if ny % 2 == 0 else 0}:
        for i in range(0, nx - 1, 2):
            y_odd += both(joint(i, j), joint(i + 1, j))
    return x_even, x_odd, y_even, y_odd


def directions():
    odd_x = lax.rem(lax.axis_index("rx"), 2)
    odd_y = lax.rem(lax.axis_index("ry"), 2)
    return 1 - odd_x, odd_x, 3 - odd_y, 2 + odd_y


def iota(shape, dim):
    return lax.broadcasted_iota(jnp.int32, shape, dim)


def hot(rows, wanted):
    return jnp.where(rows == wanted, 1.0, 0.0)


def dot(a, b):
    return jnp.dot(a, b, preferred_element_type=F32)


def dot_rows(a, b):
    return lax.dot_general(a, b, (((0,), (0,)), ((), ())), preferred_element_type=F32)


def dot_lanes(a, b):
    return lax.dot_general(a, b, (((1,), (1,)), ((), ())), preferred_element_type=F32)


def lanes(x, i, width=LANE):
    return x[:, i * width : (i + 1) * width]


def rows(x, i, height=LANE):
    return x[i * height : (i + 1) * height]


def mask_kernel(mask_ref):
    shape = mask_ref.shape
    mask_ref[...] = hot(lax.rem(iota(shape, 0), shape[1]), iota(shape, 1))


def pack_kernel(mask_ref, primal_ref, adjoint_ref, send_ref, pick_ref, *messages):
    count, sent = primal_ref.shape[1], send_ref.shape[1]
    table = jnp.concatenate(
        [jnp.broadcast_to(send_ref[pl.ds(face, 1), :], (sent, sent)) for face in directions()], axis=0
    )
    column = jnp.sum(table.astype(F32) * mask_ref[...], axis=1, keepdims=True).astype(jnp.int32)
    pick = hot(iota((4 * sent, count), 1), column).astype(BF16)
    pick_ref[...] = pick
    state = jnp.concatenate([primal_ref[...], adjoint_ref[...]], axis=0)
    packed = dot_lanes(pick, state).astype(BF16)
    for j, out_ref in enumerate(messages):
        out_ref[...] = rows(packed, j, sent)


def local_kernel(
    primal_ref,
    adjoint_ref,
    nbr_ref,
    recon_ref,
    deriv_ref,
    lift_ref,
    trace_ref,
    pick_ref,
    near_ref,
    listed_ref,
    hot_ref,
    listed_hot_ref,
    far_recon_ref,
    pair_recon_ref,
    weights_ref,
    back_ref,
    gathered_ref,
    tall_ref,
    square_ref,
    wide_ref,
    trace_pad_ref,
):
    count = nbr_ref.shape[1]
    sent = pick_ref.shape[0] // 4
    faces = directions()
    tall_ref[...] = jnp.zeros_like(tall_ref)
    for k in range(PATCH):
        tall_ref[k * MODES : (k + 1) * MODES, 0:ENR] = recon_ref[k].astype(F32)
    recon_t = tall_ref[...].T.astype(BF16)[:, 0 : PATCH * MODES]
    pair_recon_ref[...] = jnp.zeros_like(pair_recon_ref)
    for j, face in enumerate(faces):
        mine = tall_ref[pl.ds((face + 1) * MODES, MODES), :]
        far_recon_ref[:, j * MODES : (j + 1) * MODES] = mine.T.astype(BF16)
        pair_recon_ref[j * LANE : j * LANE + MODES, 0:LANE] = mine.astype(BF16)
        pair_recon_ref[j * LANE + MODES : (j + 1) * LANE, LANE:] = mine.astype(BF16)
    hots = [
        hot(iota((sent, count), 0) + (count + face * sent), nbr_ref[pl.ds(face, 1), :]).astype(BF16)
        for face in faces
    ]
    hot_ref[...] = jnp.zeros_like(hot_ref)
    for j in range(4):
        hot_ref[j * sent : (j + 1) * sent, j * count : (j + 1) * count] = hots[j]
    pick = pick_ref[...]
    listed = dot_lanes(pick, jnp.concatenate(hots, axis=0))
    source = iota((1, 4 * sent), 1) // sent
    for j in range(4):
        listed_hot_ref[j * 4 * sent : (j + 1) * 4 * sent, :] = jnp.where(source == j, listed, 0.0).astype(BF16)
    local = jnp.concatenate(
        [hot(iota((count, count), 0), nbr_ref[f : f + 1, :]).astype(BF16) for f in range(FACES)], axis=1
    )
    for i, ref in enumerate((primal_ref, adjoint_ref)):
        state = ref[...]
        found = dot(state, local).astype(BF16)
        for v in range(VARS):
            place = slice((i * VARS + v) * count, (i * VARS + v + 1) * count)
            gathered_ref[0:MODES, place] = rows(state, v, MODES)
            for f in range(FACES):
                gathered_ref[(f + 1) * MODES : (f + 2) * MODES, place] = rows(lanes(found, f), v, MODES)
    near = dot(recon_t, gathered_ref[...])
    near_ref[...] = near
    stack = jnp.concatenate([lanes(near, v) for v in range(VARS)], axis=0)
    high = stack.astype(BF16)
    low = (stack - high.astype(F32)).astype(BF16)
    listed_ref[...] = dot_lanes(pick, high) + dot_lanes(pick, low)
    wide_ref[...] = jnp.zeros_like(wide_ref)
    wide_ref[0:POINTS, 0:ENR] = lift_ref[...].astype(F32)
    trace_pad_ref[...] = jnp.zeros_like(trace_pad_ref)
    trace_pad_ref[0:POINTS, 0:ENR] = trace_ref[...]
    lift_t = wide_ref[...].T
    face = iota((1, 2 * LANE), 1) // FACEPTS
    up = pltpu.roll(lift_t, FACEPTS, 1)
    down = pltpu.roll(lift_t, 2 * LANE - FACEPTS, 1)
    blocks = []
    for a in range(3):
        half = jnp.where(face == 2 * a, 0.5, jnp.where(face == 2 * a + 1, -0.5, 0.0))
        blocks.append(lift_t * half)
    blocks.append(-0.5 * lift_t)
    for f in range(FACES):
        blocks.append(jnp.where(face == f ^ 1, down if f % 2 else up, 0.0) * 0.5)
    products = dot(jnp.concatenate(blocks, axis=0).astype(BF16), trace_pad_ref[...])
    weights_ref[...] = jnp.zeros_like(weights_ref)
    square_ref[...] = jnp.zeros_like(square_ref)
    for a in range(3):
        square_ref[0:ENR, 0:ENR] = deriv_ref[a].astype(F32)
        weights_ref[a * LANE : (a + 1) * LANE, 0:LANE] = (
            square_ref[...].T + products[a * LANE : (a + 1) * LANE]
        ).astype(BF16)
    weights_ref[3 * LANE : 4 * LANE, 0:LANE] = products[3 * LANE : 4 * LANE].astype(BF16)
    for f in range(FACES):
        across = products[(4 + f) * LANE : (5 + f) * LANE]
        place = slice((f + 1) * LANE, (f + 2) * LANE)
        row = (f // 2) * LANE
        weights_ref[row : row + LANE, place] = (-across if f % 2 else across).astype(BF16)
        weights_ref[3 * LANE : 4 * LANE, place] = across.astype(BF16)
        if f < 4:
            back_ref[f] = across.T.astype(BF16)


def listed_kernel(near_ref, hot_ref, recon_ref, a_ref, b_ref, c_ref, d_ref, *messages):
    sent = a_ref.shape[0]
    packed = jnp.concatenate([ref[:, 0 : 3 * LANE] for ref in (a_ref, b_ref, c_ref, d_ref)], axis=0)
    found = dot(hot_ref[...], packed).astype(BF16)
    left = jnp.concatenate(
        [jnp.concatenate([lanes(rows(found, j, 4 * sent), t) for j in range(4)], axis=1) for t in range(3)], axis=0
    )
    far = dot(left, recon_ref[...])
    for v in range(VARS):
        state = lanes(rows(far, v // 2, 4 * sent), v % 2) + lanes(near_ref[...], v)
        for j, out_ref in enumerate(messages):
            out_ref[:, v * LANE : (v + 1) * LANE] = rows(state, j, sent).astype(BF16)


def middle_kernel(
    near_ref,
    hot_ref,
    recon_ref,
    nbr_ref,
    weights_ref,
    back_ref,
    jacob_ref,
    dissip_ref,
    a_ref,
    b_ref,
    c_ref,
    d_ref,
    part_ref,
    coef_ref,
    right_ref,
    state_ref,
    signed_ref,
):
    count = nbr_ref.shape[1]
    packed = jnp.concatenate([ref[...] for ref in (a_ref, b_ref, c_ref, d_ref)], axis=0)
    found = dot_rows(packed, hot_ref[...]).astype(BF16)
    far = [
        jnp.concatenate(
            [
                jnp.concatenate([rows(lanes(found, j), i * VARS + v, MODES) for v in range(VARS)], axis=1)
                for j in range(4)
            ],
            axis=0,
        )
        for i in range(2)
    ]
    u = (near_ref[:, 0:WIDE] + dot(recon_ref[...], far[0])).astype(BF16)
    state_ref[...] = near_ref[:, WIDE:] + dot(recon_ref[...], far[1])
    right_ref[0:LANE, :] = u
    stack = jnp.concatenate([lanes(u, v) for v in range(VARS)], axis=0)
    local = jnp.concatenate(
        [hot(iota((count, count), 0), nbr_ref[f : f + 1, :]).astype(BF16) for f in range(FACES)], axis=1
    )
    across = dot(stack, local).astype(BF16)
    for f in range(FACES):
        for v in range(VARS):
            right_ref[(f + 1) * LANE : (f + 2) * LANE, v * count : (v + 1) * count] = rows(lanes(across, f), v)
    mixed = dot(weights_ref[...], right_ref[...])
    part = jnp.zeros((LANE, count), F32)
    for w in range(VARS):
        place = slice(w * count, (w + 1) * count)
        damped = dissip_ref[w] * state_ref[:, place]
        part = part + damped * mixed[3 * LANE :, place]
        for a in range(3):
            turned = jacob_ref[0, a, w] * state_ref[:, 0:count]
            for v in range(1, VARS):
                turned = turned + jacob_ref[v, a, w] * state_ref[:, v * count : (v + 1) * count]
            part = part + turned * mixed[a * LANE : (a + 1) * LANE, place]
            if a < 2:
                signed_ref[2 * a, :, place] = (damped + turned).astype(BF16)
                signed_ref[2 * a + 1, :, place] = (damped - turned).astype(BF16)
    for f in range(4):
        coef = dot(back_ref[f], signed_ref[f])
        for v in range(VARS):
            coef_ref[f, v * LANE : (v + 1) * LANE, :] = lanes(coef, v)
    part_ref[...] = jnp.sum(part.reshape(LANE // 8, 8, count), axis=0)


def last_kernel(part_ref, coef_ref, hot_ref, a_ref, b_ref, c_ref, d_ref, out_ref):
    packed = jnp.concatenate([ref[...] for ref in (a_ref, b_ref, c_ref, d_ref)], axis=0)
    found = dot_rows(packed, hot_ref[...])
    terms = lanes(found, 0) * coef_ref[directions()[0]]
    for j, face in enumerate(directions()):
        if j:
            terms = terms + lanes(found, j) * coef_ref[face]
    total = part_ref[...] + jnp.sum(terms.reshape(WIDE // 8, 8, terms.shape[1]), axis=0)
    out_ref[...] = 0.04 * jnp.sum(total, axis=0, keepdims=True)


def call(kernel, outs, specs=None, scratch=(), flops=10**6, moved=10**5, grant=VMEM_BYTES):
    def run(*args):
        places = specs or [pltpu.VMEM] * len(args)
        return pl.pallas_call(
            kernel,
            out_shape=outs,
            in_specs=[pl.BlockSpec(memory_space=m) for m in places],
            out_specs=jax.tree.map(lambda _: pl.BlockSpec(memory_space=pltpu.VMEM), outs),
            scratch_shapes=scratch,
            compiler_params=pltpu.CompilerParams(vmem_limit_bytes=grant),
            cost_estimate=pl.CostEstimate(flops=flops, bytes_accessed=moved, transcendentals=0),
        )(*args)

    return run


def shards(mesh, primal, adjoint, send_index, neighbours, recon, deriv, jacob, face_trace, lift, dissip):
    count, sent = primal.shape[0], send_index.shape[1]
    perms = swaps(mesh.shape["rx"], mesh.shape["ry"])
    shape, vmem, smem = jax.ShapeDtypeStruct, pltpu.VMEM, pltpu.SMEM
    message = shape((sent, WIDE), BF16)
    primal_t, adjoint_t, nbr = primal.T, adjoint.T, neighbours.T
    mask = call(mask_kernel, shape((4 * sent, sent), F32), flops=5 * 10**9)()
    pick, *first = call(pack_kernel, [shape((4 * sent, count), BF16)] + [message] * 4, flops=10**9)(
        mask, primal_t, adjoint_t, send_index
    )
    got = [lax.ppermute(m, AXES, pairs) for m, pairs in zip(first, perms)]
    near, listed, hots, listed_hots, far_recon, pair_recon, weights, back = call(
        local_kernel,
        [
            shape((LANE, 2 * WIDE), F32),
            shape((4 * sent, WIDE), F32),
            shape((4 * sent, 4 * count), BF16),
            shape((16 * sent, 4 * sent), BF16),
            shape((LANE, 4 * MODES), BF16),
            shape((4 * LANE, 2 * LANE), BF16),
            shape((4 * LANE, 7 * LANE), BF16),
            shape((4, LANE, LANE), BF16),
        ],
        scratch=[
            vmem((PATCH * MODES, 2 * WIDE), BF16),
            vmem((4 * LANE, LANE), F32),
            vmem((LANE, LANE), F32),
            vmem((2 * LANE, LANE), F32),
            vmem((2 * LANE, LANE), BF16),
        ],
        flops=10**9,
        moved=10**6,
    )(primal_t, adjoint_t, nbr, recon, deriv, lift, face_trace.T, pick)
    second = call(listed_kernel, [message] * 4)(listed, listed_hots, pair_recon, *got)
    got_more = [lax.ppermute(m, AXES, pairs) for m, pairs in zip(second, perms)]
    part, coef = call(
        middle_kernel,
        [shape((8, count), F32), shape((4, WIDE, count), F32)],
        specs=[vmem] * 6 + [smem] * 2 + [vmem] * 4,
        scratch=[vmem((7 * LANE, WIDE), BF16), vmem((LANE, WIDE), F32), vmem((4, LANE, WIDE), BF16)],
        flops=10**9,
        moved=10**6,
    )(near, hots, far_recon, nbr, weights, back, jacob.transpose(1, 0, 2), dissip, *got)
    out = call(last_kernel, shape((1, count), F32))(part, coef, hots, *got_more)
    return out.reshape(count)


def solution(mesh):
    rows = P(AXES, None)
    return jax.shard_map(
        functools.partial(shards, mesh),
        mesh=mesh,
        in_specs=(rows, rows, rows, rows, P(), P(), P(), P(), P(), P()),
        out_specs=P(AXES),
        check_vma=False,
    )
```

```python
import functools

import jax
import jax.numpy as jnp
from jax import lax
from jax.experimental import pallas as pl
from jax.experimental.pallas import tpu as pltpu
from jax.sharding import PartitionSpec as P

VARS = 5
MODES = 64
ENR = 125
FACEPTS = 25
FACES = 6
PATCH = 7
LANE = 128
WIDE = VARS * LANE
FIELD = VARS * MODES
POINTS = FACES * FACEPTS
AXES = ("rx", "ry")
F32 = jnp.float32
BF16 = jnp.bfloat16
VMEM_BYTES = 16 * 1024 * 1024


def swaps(nx, ny):
    def joint(i, j):
        return i * ny + j

    def both(a, b):
        return [(a, b), (b, a)]

    x_even, x_odd, y_even, y_odd = [], [], [], []
    for j in range(ny):
        for i in range(0, nx - 1, 2):
            x_even += both(joint(i, j), joint(i + 1, j))
        for i in range(1, nx - 1, 2):
            x_odd += both(joint(i, j), joint(i + 1, j))
    for i in range(nx):
        for j in range(0, ny - 1, 2):
            y_even += both(joint(i, j), joint(i, j + 1))
        for j in range(1, ny - 1, 2):
            y_odd += both(joint(i, j), joint(i, j + 1))
    for i in {0, nx - 1 if nx % 2 == 0 else 0}:
        for j in range(0, ny - 1, 2):
            x_odd += both(joint(i, j), joint(i, j + 1))
    for j in {0, ny - 1 if ny % 2 == 0 else 0}:
        for i in range(0, nx - 1, 2):
            y_odd += both(joint(i, j), joint(i + 1, j))
    return y_even, y_odd, x_odd, x_even


def directions():
    odd_x = lax.rem(lax.axis_index("rx"), 2)
    odd_y = lax.rem(lax.axis_index("ry"), 2)
    return 3 - odd_y, 2 + odd_y, odd_x, 1 - odd_x


def iota(shape, dim):
    return lax.broadcasted_iota(jnp.int32, shape, dim)


def hot(rows, wanted):
    return jnp.where(rows == wanted, 1.0, 0.0)


def dot(a, b):
    return jnp.dot(a, b, preferred_element_type=F32)


def dot_rows(a, b):
    return lax.dot_general(a, b, (((0,), (0,)), ((), ())), preferred_element_type=F32)


def dot_lanes(a, b):
    return lax.dot_general(a, b, (((1,), (1,)), ((), ())), preferred_element_type=F32)


def lanes(x, i, width=LANE):
    return x[:, i * width : (i + 1) * width]


def rows(x, i, height=LANE):
    return x[i * height : (i + 1) * height]


def mask_kernel(mask_ref):
    shape = mask_ref.shape
    mask_ref[...] = hot(lax.rem(iota(shape, 0), shape[1]), iota(shape, 1))


def pack_kernel(mask_ref, primal_ref, adjoint_ref, send_ref, pick_ref, *messages):
    count, sent = primal_ref.shape[1], send_ref.shape[1]
    table = jnp.concatenate(
        [jnp.broadcast_to(send_ref[pl.ds(face, 1), :], (sent, sent)) for face in directions()], axis=0
    )
    column = jnp.sum(table.astype(F32) * mask_ref[...], axis=1, keepdims=True).astype(jnp.int32)
    pick = hot(iota((4 * sent, count), 1), column).astype(BF16)
    pick_ref[...] = pick
    state = jnp.concatenate([primal_ref[...], adjoint_ref[...]], axis=0)
    packed = dot_lanes(pick, state).astype(BF16)
    for j, out_ref in enumerate(messages):
        out_ref[...] = rows(packed, j, sent)


def local_kernel(
    primal_ref,
    adjoint_ref,
    nbr_ref,
    recon_ref,
    deriv_ref,
    lift_ref,
    trace_ref,
    pick_ref,
    jacob_ref,
    dissip_ref,
    near_ref,
    listed_ref,
    hot_ref,
    listed_hot_ref,
    far_recon_ref,
    pair_recon_ref,
    inner_ref,
    pairs_ref,
    back_ref,
    local_ref,
    factors_ref,
    gathered_ref,
    tall_ref,
    square_ref,
    wide_ref,
    trace_pad_ref,
):
    count = nbr_ref.shape[1]
    sent = pick_ref.shape[0] // 4
    faces = directions()
    tall_ref[...] = jnp.zeros_like(tall_ref)
    for k in range(PATCH):
        tall_ref[k * MODES : (k + 1) * MODES, 0:ENR] = recon_ref[k].astype(F32)
    recon_t = tall_ref[...].T.astype(BF16)[:, 0 : PATCH * MODES]
    pair_recon_ref[...] = jnp.zeros_like(pair_recon_ref)
    for j, face in enumerate(faces):
        mine = tall_ref[pl.ds((face + 1) * MODES, MODES), :]
        far_recon_ref[:, j * MODES : (j + 1) * MODES] = mine.T.astype(BF16)
        pair_recon_ref[j * LANE : j * LANE + MODES, 0:LANE] = mine.astype(BF16)
        pair_recon_ref[j * LANE + MODES : (j + 1) * LANE, LANE:] = mine.astype(BF16)
    hots = [
        hot(iota((sent, count), 0) + (count + face * sent), nbr_ref[pl.ds(face, 1), :]).astype(BF16)
        for face in faces
    ]
    hot_ref[...] = jnp.zeros_like(hot_ref)
    for j in range(4):
        hot_ref[j * sent : (j + 1) * sent, j * count : (j + 1) * count] = hots[j]
    pick = pick_ref[...]
    listed = dot_lanes(pick, jnp.concatenate(hots, axis=0))
    source = iota((1, 4 * sent), 1) // sent
    for j in range(4):
        listed_hot_ref[j * 4 * sent : (j + 1) * 4 * sent, :] = jnp.where(source == j, listed, 0.0).astype(BF16)
    local = jnp.concatenate(
        [hot(iota((count, count), 0), nbr_ref[f : f + 1, :]).astype(BF16) for f in range(FACES)], axis=1
    )
    local_ref[...] = local
    for i, ref in enumerate((primal_ref, adjoint_ref)):
        state = ref[...]
        found = dot(state, local).astype(BF16)
        for v in range(VARS):
            place = slice((i * VARS + v) * count, (i * VARS + v + 1) * count)
            gathered_ref[0:MODES, place] = rows(state, v, MODES)
            for f in range(FACES):
                gathered_ref[(f + 1) * MODES : (f + 2) * MODES, place] = rows(lanes(found, f), v, MODES)
    near = dot(recon_t, gathered_ref[...])
    near_ref[...] = near
    stack = jnp.concatenate([lanes(near, v) for v in range(VARS)], axis=0)
    high = stack.astype(BF16)
    low = (stack - high.astype(F32)).astype(BF16)
    listed_ref[...] = dot_lanes(pick, high) + dot_lanes(pick, low)
    wide_ref[...] = jnp.zeros_like(wide_ref)
    wide_ref[0:POINTS, 0:ENR] = lift_ref[...].astype(F32)
    trace_pad_ref[...] = jnp.zeros_like(trace_pad_ref)
    trace_pad_ref[0:POINTS, 0:ENR] = trace_ref[...]
    lift_t = wide_ref[...].T
    face = iota((1, 2 * LANE), 1) // FACEPTS
    up = pltpu.roll(lift_t, FACEPTS, 1)
    down = pltpu.roll(lift_t, 2 * LANE - FACEPTS, 1)
    blocks = []
    for a in range(3):
        half = jnp.where(face == 2 * a, 0.5, jnp.where(face == 2 * a + 1, -0.5, 0.0))
        blocks.append(lift_t * half)
    blocks.append(-0.5 * lift_t)
    for f in range(FACES):
        blocks.append(jnp.where(face == f ^ 1, down if f % 2 else up, 0.0) * 0.5)
    products = dot(jnp.concatenate(blocks, axis=0).astype(BF16), trace_pad_ref[...])
    square_ref[...] = jnp.zeros_like(square_ref)
    for a in range(3):
        square_ref[0:ENR, 0:ENR] = deriv_ref[a].astype(F32)
        inner_ref[a * LANE : (a + 1) * LANE, :] = (square_ref[...].T + rows(products, a)).astype(BF16)
    inner_ref[3 * LANE :, :] = rows(products, 3).astype(BF16)
    for f in range(FACES):
        across = rows(products, 4 + f)
        place = slice((f % 2) * LANE, (f % 2 + 1) * LANE)
        pairs_ref[f // 2, 0:LANE, place] = (-across if f % 2 else across).astype(BF16)
        pairs_ref[f // 2, LANE:, place] = across.astype(BF16)
        if f < 4:
            back_ref[f] = across.T.astype(BF16)
    for w in range(VARS):
        for v in range(VARS):
            at = (w * VARS + v) * 3
            factors_ref[at : at + 3, :] = jnp.broadcast_to(jacob_ref[v][:, w : w + 1], (3, count))
        at = 15 * VARS + w
        factors_ref[at : at + 1, :] = jnp.broadcast_to(dissip_ref[:, w : w + 1], (1, count))


def listed_kernel(near_ref, hot_ref, recon_ref, a_ref, b_ref, c_ref, d_ref, *messages):
    sent = a_ref.shape[0]
    packed = jnp.concatenate([ref[:, 0 : 3 * LANE] for ref in (a_ref, b_ref, c_ref, d_ref)], axis=0)
    found = dot(hot_ref[...], packed).astype(BF16)
    left = jnp.concatenate(
        [jnp.concatenate([lanes(rows(found, j, 4 * sent), t) for j in range(4)], axis=1) for t in range(3)], axis=0
    )
    far = dot(left, recon_ref[...])
    for v in range(VARS):
        state = lanes(rows(far, v // 2, 4 * sent), v % 2) + lanes(near_ref[...], v)
        for j, out_ref in enumerate(messages):
            out_ref[:, v * LANE : (v + 1) * LANE] = rows(state, j, sent).astype(BF16)


def middle_kernel(
    near_ref,
    hot_ref,
    recon_ref,
    local_ref,
    inner_ref,
    pairs_ref,
    back_ref,
    factors_ref,
    a_ref,
    b_ref,
    c_ref,
    d_ref,
    part_ref,
    coef_ref,
    right_ref,
    state_ref,
    signed_ref,
):
    count = local_ref.shape[0]
    packed = jnp.concatenate([ref[...] for ref in (a_ref, b_ref, c_ref, d_ref)], axis=0)
    found = dot_rows(packed, hot_ref[...]).astype(BF16)
    far = [
        jnp.concatenate(
            [
                jnp.concatenate([rows(lanes(found, j), i * VARS + v, MODES) for v in range(VARS)], axis=1)
                for j in range(4)
            ],
            axis=0,
        )
        for i in range(2)
    ]
    u = (near_ref[:, 0:WIDE] + dot(recon_ref[...], far[0])).astype(BF16)
    state_ref[...] = near_ref[:, WIDE:] + dot(recon_ref[...], far[1])
    stack = jnp.concatenate([lanes(u, v) for v in range(VARS)], axis=0)
    across = dot(stack, local_ref[...]).astype(BF16)
    for f in range(FACES):
        for v in range(VARS):
            right_ref[f * LANE : (f + 1) * LANE, v * count : (v + 1) * count] = rows(lanes(across, f), v)
    mixed = dot(inner_ref[...], u)
    turns = [dot(pairs_ref[a], right_ref[2 * a * LANE : 2 * (a + 1) * LANE, :]) for a in range(3)]
    total = jnp.zeros((8, count), F32)
    height = 32
    for c in range(LANE // height):
        at = slice(c * height, (c + 1) * height)
        low = slice(LANE + c * height, LANE + (c + 1) * height)
        z = [state_ref[at, v * count : (v + 1) * count] for v in range(VARS)]
        part = jnp.zeros((height, count), F32)
        for w in range(VARS):
            place = slice(w * count, (w + 1) * count)
            damped = factors_ref[15 * VARS + w : 15 * VARS + w + 1, :] * z[w]
            bottom = slice(3 * LANE + c * height, 3 * LANE + (c + 1) * height)
            whole = mixed[bottom, place] + turns[0][low, place] + turns[1][low, place] + turns[2][low, place]
            part = part + damped * whole
            for a in range(3):
                row = w * VARS * 3 + a
                turned = factors_ref[row : row + 1, :] * z[0]
                for v in range(1, VARS):
                    turned = turned + factors_ref[row + 3 * v : row + 3 * v + 1, :] * z[v]
                side = slice(a * LANE + c * height, a * LANE + (c + 1) * height)
                part = part + turned * (mixed[side, place] + turns[a][at, place])
                if a < 2:
                    signed_ref[2 * a, at, place] = (damped + turned).astype(BF16)
                    signed_ref[2 * a + 1, at, place] = (damped - turned).astype(BF16)
        total = total + jnp.sum(part.reshape(height // 8, 8, count), axis=0)
    for j, face in enumerate(directions()):
        coef = dot(back_ref[face], signed_ref[face]).astype(BF16)
        for v in range(VARS):
            coef_ref[v * LANE : (v + 1) * LANE, j * count : (j + 1) * count] = lanes(coef, v)
    part_ref[...] = total


def last_kernel(part_ref, coef_ref, hot_ref, a_ref, b_ref, c_ref, d_ref, out_ref):
    packed = jnp.concatenate([ref[...] for ref in (a_ref, b_ref, c_ref, d_ref)], axis=0)
    terms = dot(packed, coef_ref[...]) * hot_ref[...].astype(F32)
    sums = jnp.sum(terms, axis=0, keepdims=True)
    total = jnp.sum(part_ref[...], axis=0, keepdims=True)
    for j in range(4):
        total = total + lanes(sums, j)
    out_ref[...] = 0.04 * total


def call(kernel, outs, specs=None, scratch=(), flops=10**6, moved=10**5, grant=VMEM_BYTES):
    def run(*args):
        places = specs or [pltpu.VMEM] * len(args)
        return pl.pallas_call(
            kernel,
            out_shape=outs,
            in_specs=[pl.BlockSpec(memory_space=m) for m in places],
            out_specs=jax.tree.map(lambda _: pl.BlockSpec(memory_space=pltpu.VMEM), outs),
            scratch_shapes=scratch,
            compiler_params=pltpu.CompilerParams(vmem_limit_bytes=grant),
            cost_estimate=pl.CostEstimate(flops=flops, bytes_accessed=moved, transcendentals=0),
        )(*args)

    return run


def shards(mesh, primal, adjoint, send_index, neighbours, recon, deriv, jacob, face_trace, lift, dissip):
    count, sent = primal.shape[0], send_index.shape[1]
    perms = swaps(mesh.shape["rx"], mesh.shape["ry"])
    shape, vmem, smem = jax.ShapeDtypeStruct, pltpu.VMEM, pltpu.SMEM
    message = shape((sent, WIDE), BF16)
    primal_t, adjoint_t, nbr = primal.T, adjoint.T, neighbours.T
    mask = call(mask_kernel, shape((4 * sent, sent), F32), flops=5 * 10**9)()
    pick, *first = call(pack_kernel, [shape((4 * sent, count), BF16)] + [message] * 4, flops=10**9)(
        mask, primal_t, adjoint_t, send_index
    )
    got = [lax.ppermute(m, AXES, pairs) for m, pairs in zip(first, perms)]
    near, listed, hots, listed_hots, far_recon, pair_recon, inner, pairs, back, local, factors = call(
        local_kernel,
        [
            shape((LANE, 2 * WIDE), F32),
            shape((4 * sent, WIDE), F32),
            shape((4 * sent, 4 * count), BF16),
            shape((16 * sent, 4 * sent), BF16),
            shape((LANE, 4 * MODES), BF16),
            shape((4 * LANE, 2 * LANE), BF16),
            shape((4 * LANE, LANE), BF16),
            shape((3, 2 * LANE, 2 * LANE), BF16),
            shape((4, LANE, LANE), BF16),
            shape((count, FACES * count), BF16),
            shape((16 * VARS, count), F32),
        ],
        scratch=[
            vmem((PATCH * MODES, 2 * WIDE), BF16),
            vmem((4 * LANE, LANE), F32),
            vmem((LANE, LANE), F32),
            vmem((2 * LANE, LANE), F32),
            vmem((2 * LANE, LANE), BF16),
        ],
        flops=3 * 10**9,
        moved=10**6,
    )(primal_t, adjoint_t, nbr, recon, deriv, lift, face_trace.T, pick, jacob.transpose(1, 0, 2), dissip[None])
    second = call(listed_kernel, [message] * 4)(listed, listed_hots, pair_recon, *got)
    got_more = [lax.ppermute(m, AXES, pairs) for m, pairs in zip(second, perms)]
    part, coef = call(
        middle_kernel,
        [shape((8, count), F32), shape((WIDE, 4 * count), BF16)],
        scratch=[vmem((FACES * LANE, WIDE), BF16), vmem((LANE, WIDE), F32), vmem((4, LANE, WIDE), BF16)],
        flops=10**9,
        moved=10**6,
    )(near, hots, far_recon, local, inner, pairs, back, factors, *got)
    out = call(last_kernel, shape((1, count), F32))(part, coef, hots, *got_more)
    return out.reshape(count)


def solution(mesh):
    rows = P(AXES, None)
    return jax.shard_map(
        functools.partial(shards, mesh),
        mesh=mesh,
        in_specs=(rows, rows, rows, rows, P(), P(), P(), P(), P(), P()),
        out_specs=P(AXES),
        check_vma=False,
    )
```

```python
import functools

import jax
import jax.numpy as jnp
from jax import lax
from jax.experimental import pallas as pl
from jax.experimental.pallas import tpu as pltpu
from jax.sharding import PartitionSpec as P

VARS = 5
MODES = 64
ENR = 125
FACEPTS = 25
FACES = 6
PATCH = 7
LANE = 128
WIDE = VARS * LANE
FIELD = VARS * MODES
POINTS = FACES * FACEPTS
AXES = ("rx", "ry")
LATER = (1, 2, 0, 3)
F32 = jnp.float32
BF16 = jnp.bfloat16
VMEM_BYTES = 16 * 1024 * 1024


def swaps(nx, ny):
    def joint(i, j):
        return i * ny + j

    def both(a, b):
        return [(a, b), (b, a)]

    x_even, x_odd, y_even, y_odd = [], [], [], []
    for j in range(ny):
        for i in range(0, nx - 1, 2):
            x_even += both(joint(i, j), joint(i + 1, j))
        for i in range(1, nx - 1, 2):
            x_odd += both(joint(i, j), joint(i + 1, j))
    for i in range(nx):
        for j in range(0, ny - 1, 2):
            y_even += both(joint(i, j), joint(i, j + 1))
        for j in range(1, ny - 1, 2):
            y_odd += both(joint(i, j), joint(i, j + 1))
    for i in {0, nx - 1 if nx % 2 == 0 else 0}:
        for j in range(0, ny - 1, 2):
            x_odd += both(joint(i, j), joint(i, j + 1))
    for j in {0, ny - 1 if ny % 2 == 0 else 0}:
        for i in range(0, nx - 1, 2):
            y_odd += both(joint(i, j), joint(i + 1, j))
    return y_odd, y_even, x_odd, x_even


def directions():
    odd_x = lax.rem(lax.axis_index("rx"), 2)
    odd_y = lax.rem(lax.axis_index("ry"), 2)
    return 2 + odd_y, 3 - odd_y, odd_x, 1 - odd_x


def iota(shape, dim):
    return lax.broadcasted_iota(jnp.int32, shape, dim)


def hot(rows, wanted):
    return jnp.where(rows == wanted, 1.0, 0.0)


def dot(a, b):
    return jnp.dot(a, b, preferred_element_type=F32)


def dot_rows(a, b):
    return lax.dot_general(a, b, (((0,), (0,)), ((), ())), preferred_element_type=F32)


def dot_lanes(a, b):
    return lax.dot_general(a, b, (((1,), (1,)), ((), ())), preferred_element_type=F32)


def lanes(x, i, width=LANE):
    return x[:, i * width : (i + 1) * width]


def rows(x, i, height=LANE):
    return x[i * height : (i + 1) * height]


def mask_kernel(mask_ref):
    shape = mask_ref.shape
    mask_ref[...] = hot(lax.rem(iota(shape, 0), shape[1]), iota(shape, 1))


def pack_kernel(mask_ref, primal_ref, adjoint_ref, send_ref, pick_ref, *messages):
    count, sent = primal_ref.shape[1], send_ref.shape[1]
    table = jnp.concatenate(
        [jnp.broadcast_to(send_ref[pl.ds(face, 1), :], (sent, sent)) for face in directions()], axis=0
    )
    column = jnp.sum(table.astype(F32) * mask_ref[...], axis=1, keepdims=True).astype(jnp.int32)
    pick = hot(iota((4 * sent, count), 1), column).astype(BF16)
    pick_ref[...] = pick
    state = jnp.concatenate([primal_ref[...], adjoint_ref[...]], axis=0)
    packed = dot_lanes(pick, state).astype(BF16)
    for j, out_ref in enumerate(messages):
        out_ref[...] = rows(packed, j, sent)


def local_kernel(
    primal_ref,
    adjoint_ref,
    nbr_ref,
    recon_ref,
    deriv_ref,
    lift_ref,
    trace_ref,
    pick_ref,
    jacob_ref,
    dissip_ref,
    near_ref,
    listed_ref,
    hot_ref,
    listed_hot_ref,
    far_recon_ref,
    pair_recon_ref,
    inner_ref,
    pairs_ref,
    back_ref,
    local_ref,
    factors_ref,
    gathered_ref,
    tall_ref,
    square_ref,
    wide_ref,
    trace_pad_ref,
):
    count = nbr_ref.shape[1]
    sent = pick_ref.shape[0] // 4
    faces = directions()
    tall_ref[...] = jnp.zeros_like(tall_ref)
    for k in range(PATCH):
        tall_ref[k * MODES : (k + 1) * MODES, 0:ENR] = recon_ref[k].astype(F32)
    recon_t = tall_ref[...].T.astype(BF16)[:, 0 : PATCH * MODES]
    pair_recon_ref[...] = jnp.zeros_like(pair_recon_ref)
    for j, face in enumerate(faces):
        mine = tall_ref[pl.ds((face + 1) * MODES, MODES), :]
        far_recon_ref[:, j * MODES : (j + 1) * MODES] = mine.T.astype(BF16)
        pair_recon_ref[j * LANE : j * LANE + MODES, 0:LANE] = mine.astype(BF16)
        pair_recon_ref[j * LANE + MODES : (j + 1) * LANE, LANE:] = mine.astype(BF16)
    hots = [
        hot(iota((sent, count), 0) + (count + face * sent), nbr_ref[pl.ds(face, 1), :]).astype(BF16)
        for face in faces
    ]
    hot_ref[...] = jnp.zeros_like(hot_ref)
    for j in range(4):
        hot_ref[j * sent : (j + 1) * sent, j * count : (j + 1) * count] = hots[j]
    pick = pick_ref[...]
    listed = dot_lanes(pick, jnp.concatenate(hots, axis=0))
    source = iota((1, 4 * sent), 1) // sent
    for j in range(4):
        listed_hot_ref[j * 4 * sent : (j + 1) * 4 * sent, :] = jnp.where(source == j, listed, 0.0).astype(BF16)
    local = jnp.concatenate(
        [hot(iota((count, count), 0), nbr_ref[f : f + 1, :]).astype(BF16) for f in range(FACES)], axis=1
    )
    local_ref[...] = local
    for i, ref in enumerate((primal_ref, adjoint_ref)):
        state = ref[...]
        found = dot(state, local).astype(BF16)
        for v in range(VARS):
            place = slice((i * VARS + v) * count, (i * VARS + v + 1) * count)
            gathered_ref[0:MODES, place] = rows(state, v, MODES)
            for f in range(FACES):
                gathered_ref[(f + 1) * MODES : (f + 2) * MODES, place] = rows(lanes(found, f), v, MODES)
    near = dot(recon_t, gathered_ref[...])
    near_ref[...] = near
    stack = jnp.concatenate([lanes(near, v) for v in range(VARS)], axis=0)
    high = stack.astype(BF16)
    low = (stack - high.astype(F32)).astype(BF16)
    listed_ref[...] = dot_lanes(pick, high) + dot_lanes(pick, low)
    wide_ref[...] = jnp.zeros_like(wide_ref)
    wide_ref[0:POINTS, 0:ENR] = lift_ref[...].astype(F32)
    trace_pad_ref[...] = jnp.zeros_like(trace_pad_ref)
    trace_pad_ref[0:POINTS, 0:ENR] = trace_ref[...]
    lift_t = wide_ref[...].T
    face = iota((1, 2 * LANE), 1) // FACEPTS
    up = pltpu.roll(lift_t, FACEPTS, 1)
    down = pltpu.roll(lift_t, 2 * LANE - FACEPTS, 1)
    blocks = []
    for a in range(3):
        half = jnp.where(face == 2 * a, 0.5, jnp.where(face == 2 * a + 1, -0.5, 0.0))
        blocks.append(lift_t * half)
    blocks.append(-0.5 * lift_t)
    for f in range(FACES):
        blocks.append(jnp.where(face == f ^ 1, down if f % 2 else up, 0.0) * 0.5)
    products = dot(jnp.concatenate(blocks, axis=0).astype(BF16), trace_pad_ref[...])
    square_ref[...] = jnp.zeros_like(square_ref)
    for a in range(3):
        square_ref[0:ENR, 0:ENR] = deriv_ref[a].astype(F32)
        inner_ref[a * LANE : (a + 1) * LANE, :] = (square_ref[...].T + rows(products, a)).astype(BF16)
    inner_ref[3 * LANE :, :] = rows(products, 3).astype(BF16)
    for f in range(FACES):
        across = rows(products, 4 + f)
        place = slice((f % 2) * LANE, (f % 2 + 1) * LANE)
        pairs_ref[f // 2, 0:LANE, place] = (-across if f % 2 else across).astype(BF16)
        pairs_ref[f // 2, LANE:, place] = across.astype(BF16)
        if f < 4:
            back_ref[f] = across.T.astype(BF16)
    for w in range(VARS):
        for v in range(VARS):
            at = (w * VARS + v) * 3
            factors_ref[at : at + 3, :] = jnp.broadcast_to(jacob_ref[v][:, w : w + 1], (3, count))
        at = 15 * VARS + w
        factors_ref[at : at + 1, :] = jnp.broadcast_to(dissip_ref[:, w : w + 1], (1, count))


def listed_kernel(near_ref, hot_ref, recon_ref, a_ref, b_ref, c_ref, d_ref, *messages):
    sent = a_ref.shape[0]
    packed = jnp.concatenate([ref[:, 0 : 3 * LANE] for ref in (a_ref, b_ref, c_ref, d_ref)], axis=0)
    found = dot(hot_ref[...], packed).astype(BF16)
    left = jnp.concatenate(
        [jnp.concatenate([lanes(rows(found, j, 4 * sent), t) for j in range(4)], axis=1) for t in range(3)], axis=0
    )
    far = dot(left, recon_ref[...])
    for v in range(VARS):
        state = lanes(rows(far, v // 2, 4 * sent), v % 2) + lanes(near_ref[...], v)
        for j, out_ref in enumerate(messages):
            out_ref[:, v * LANE : (v + 1) * LANE] = rows(state, j, sent).astype(BF16)


def middle_kernel(
    near_ref,
    hot_ref,
    recon_ref,
    local_ref,
    inner_ref,
    pairs_ref,
    back_ref,
    factors_ref,
    a_ref,
    b_ref,
    c_ref,
    d_ref,
    part_ref,
    coef_ref,
    right_ref,
    state_ref,
    signed_ref,
):
    count = local_ref.shape[0]
    packed = jnp.concatenate([ref[...] for ref in (a_ref, b_ref, c_ref, d_ref)], axis=0)
    found = dot_rows(packed, hot_ref[...]).astype(BF16)
    far = [
        jnp.concatenate(
            [
                jnp.concatenate([rows(lanes(found, j), i * VARS + v, MODES) for v in range(VARS)], axis=1)
                for j in range(4)
            ],
            axis=0,
        )
        for i in range(2)
    ]
    u = (near_ref[:, 0:WIDE] + dot(recon_ref[...], far[0])).astype(BF16)
    state_ref[...] = near_ref[:, WIDE:] + dot(recon_ref[...], far[1])
    stack = jnp.concatenate([lanes(u, v) for v in range(VARS)], axis=0)
    across = dot(stack, local_ref[...]).astype(BF16)
    for f in range(FACES):
        for v in range(VARS):
            right_ref[f * LANE : (f + 1) * LANE, v * count : (v + 1) * count] = rows(lanes(across, f), v)
    mixed = dot(inner_ref[...], u)
    turns = [dot(pairs_ref[a], right_ref[2 * a * LANE : 2 * (a + 1) * LANE, :]) for a in range(3)]
    total = jnp.zeros((8, count), F32)
    height = 32
    for c in range(LANE // height):
        at = slice(c * height, (c + 1) * height)
        low = slice(LANE + c * height, LANE + (c + 1) * height)
        z = [state_ref[at, v * count : (v + 1) * count] for v in range(VARS)]
        part = jnp.zeros((height, count), F32)
        for w in range(VARS):
            place = slice(w * count, (w + 1) * count)
            damped = factors_ref[15 * VARS + w : 15 * VARS + w + 1, :] * z[w]
            bottom = slice(3 * LANE + c * height, 3 * LANE + (c + 1) * height)
            whole = mixed[bottom, place] + turns[0][low, place] + turns[1][low, place] + turns[2][low, place]
            part = part + damped * whole
            for a in range(3):
                row = w * VARS * 3 + a
                turned = factors_ref[row : row + 1, :] * z[0]
                for v in range(1, VARS):
                    turned = turned + factors_ref[row + 3 * v : row + 3 * v + 1, :] * z[v]
                side = slice(a * LANE + c * height, a * LANE + (c + 1) * height)
                part = part + turned * (mixed[side, place] + turns[a][at, place])
                if a < 2:
                    signed_ref[2 * a, at, place] = (damped + turned).astype(BF16)
                    signed_ref[2 * a + 1, at, place] = (damped - turned).astype(BF16)
        total = total + jnp.sum(part.reshape(height // 8, 8, count), axis=0)
    for j, face in enumerate(directions()):
        coef = dot(back_ref[face], signed_ref[face]).astype(BF16)
        for v in range(VARS):
            coef_ref[v * LANE : (v + 1) * LANE, j * count : (j + 1) * count] = lanes(coef, v)
    part_ref[...] = total


def last_kernel(part_ref, coef_ref, hot_ref, *refs):
    out_ref = refs[4]
    packed = jnp.concatenate([refs[LATER.index(j)][...] for j in range(4)], axis=0)
    terms = dot(packed, coef_ref[...]) * hot_ref[...].astype(F32)
    sums = jnp.sum(terms, axis=0, keepdims=True)
    total = jnp.sum(part_ref[...], axis=0, keepdims=True)
    for j in range(4):
        total = total + lanes(sums, j)
    out_ref[...] = 0.04 * total


def call(kernel, outs, specs=None, scratch=(), flops=10**6, moved=10**5, grant=VMEM_BYTES):
    def run(*args):
        places = specs or [pltpu.VMEM] * len(args)
        return pl.pallas_call(
            kernel,
            out_shape=outs,
            in_specs=[pl.BlockSpec(memory_space=m) for m in places],
            out_specs=jax.tree.map(lambda _: pl.BlockSpec(memory_space=pltpu.VMEM), outs),
            scratch_shapes=scratch,
            compiler_params=pltpu.CompilerParams(vmem_limit_bytes=grant),
            cost_estimate=pl.CostEstimate(flops=flops, bytes_accessed=moved, transcendentals=0),
        )(*args)

    return run


def shards(mesh, primal, adjoint, send_index, neighbours, recon, deriv, jacob, face_trace, lift, dissip):
    count, sent = primal.shape[0], send_index.shape[1]
    perms = swaps(mesh.shape["rx"], mesh.shape["ry"])
    shape, vmem, smem = jax.ShapeDtypeStruct, pltpu.VMEM, pltpu.SMEM
    message = shape((sent, WIDE), BF16)
    primal_t, adjoint_t, nbr = primal.T, adjoint.T, neighbours.T
    mask = call(mask_kernel, shape((4 * sent, sent), F32), flops=5 * 10**9)()
    pick, *first = call(pack_kernel, [shape((4 * sent, count), BF16)] + [message] * 4, flops=10**9)(
        mask, primal_t, adjoint_t, send_index
    )
    got = [lax.ppermute(m, AXES, pairs) for m, pairs in zip(first, perms)]
    near, listed, hots, listed_hots, far_recon, pair_recon, inner, pairs, back, local, factors = call(
        local_kernel,
        [
            shape((LANE, 2 * WIDE), F32),
            shape((4 * sent, WIDE), F32),
            shape((4 * sent, 4 * count), BF16),
            shape((16 * sent, 4 * sent), BF16),
            shape((LANE, 4 * MODES), BF16),
            shape((4 * LANE, 2 * LANE), BF16),
            shape((4 * LANE, LANE), BF16),
            shape((3, 2 * LANE, 2 * LANE), BF16),
            shape((4, LANE, LANE), BF16),
            shape((count, FACES * count), BF16),
            shape((16 * VARS, count), F32),
        ],
        scratch=[
            vmem((PATCH * MODES, 2 * WIDE), BF16),
            vmem((4 * LANE, LANE), F32),
            vmem((LANE, LANE), F32),
            vmem((2 * LANE, LANE), F32),
            vmem((2 * LANE, LANE), BF16),
        ],
        flops=3 * 10**9,
        moved=10**6,
    )(primal_t, adjoint_t, nbr, recon, deriv, lift, face_trace.T, pick, jacob.transpose(1, 0, 2), dissip[None])
    second = call(listed_kernel, [message] * 4)(listed, listed_hots, pair_recon, *got)
    got_more = [lax.ppermute(second[j], AXES, perms[j]) for j in LATER]
    part, coef = call(
        middle_kernel,
        [shape((8, count), F32), shape((WIDE, 4 * count), BF16)],
        scratch=[vmem((FACES * LANE, WIDE), BF16), vmem((LANE, WIDE), F32), vmem((4, LANE, WIDE), BF16)],
        flops=10**9,
        moved=10**6,
    )(near, hots, far_recon, local, inner, pairs, back, factors, *got)
    out = call(last_kernel, shape((1, count), F32))(part, coef, hots, *got_more)
    return out.reshape(count)


def solution(mesh):
    rows = P(AXES, None)
    return jax.shard_map(
        functools.partial(shards, mesh),
        mesh=mesh,
        in_specs=(rows, rows, rows, rows, P(), P(), P(), P(), P(), P()),
        out_specs=P(AXES),
        check_vma=False,
    )
```
